32 devices in a mesh: mem: 2 (over x), tile: 16 (over z, y, core).
Axes of the slice: x: 2, y: 2, z: 4, core: 2. Of those that a mesh axis runs over, the one named last changes fastest.
Arguments:
- prior_members: bfloat16 [256, 10, 32768], P('mem', None, 'tile'), may hold values from -6 to 6
- members_in_reading_space: bfloat16 [256, 131072], P('mem', 'tile'), may hold values from -6 to 6
- measured_values: float32 [131072], P('tile'), may hold values from -6 to 6
- obs_precision_weights: float32 [131072], P('tile'), may hold values from 0.5 to 4
- valid_reading_numbers: int32 [1024], P('tile'), may hold values from 1 to 128, as said below
- neighbour_lists: int32 [256, 8], P('tile'), may hold values from 0 to 1023, as said below
Outputs:
- analysis: bfloat16 [256, 10, 32768], P('mem', None, 'tile')
The draws below stay inside these ranges and needn't reach their ends.
Inputs may be any that keep to these rules, and one draw needn't show every extreme that they name: `valid_reading_numbers`: every block count is at least 1; some block has 128 valid observations and some has 1. `neighbour_lists`: each row lists 8 different observation blocks. Column block b lies on tile b // 16; every block it lists lies on that tile or on one of the two tiles beside it, that is, in blocks (b // 16 - 1) * 64 to (b // 16 + 2) * 64 - 1.
All inputs are finite; a program needn't handle non-finite values.
Results may differ from the reference program's by a relative error of at most 0.0064.
Values may be sent and summed in bfloat16 or wider, within the bound.
A program may use at most 128 MiB of HBM per device.

```python
import math
import jax
import jax.numpy as jnp
from jax import lax

MEMBER_NUMBER = 256
HEIGHT_LAYERS = 10
CBW = 128
OBW = 128
NLOC = 8
NSTEPS = 3
OB_DEV = 64
CB_DEV = 16
GRID_POINTS = 32768
NCB = 256
NOB = 1024
NOBS = 131072


def draw_prior_members(key, part):
    offset_key = jax.random.fold_in(key, 3301)
    spread_key = jax.random.fold_in(key, 3302)
    offset = jax.random.uniform(offset_key, (1, HEIGHT_LAYERS, GRID_POINTS), jnp.float32, -1.0, 1.0)
    spread_part = jax.random.truncated_normal(spread_key, -5.0, 5.0, (MEMBER_NUMBER, HEIGHT_LAYERS, GRID_POINTS), jnp.float32)
    return (spread_part + offset).astype(jnp.bfloat16)


def draw_members_in_reading_space(key, part):
    leading_key = jax.random.fold_in(key, 7171)
    partner_key = jax.random.fold_in(key, 7172)
    half_count = MEMBER_NUMBER // 2
    leading = jax.random.truncated_normal(leading_key, -4.0, 4.0, (half_count, NOBS), jnp.float32)
    partner_own = jax.random.truncated_normal(partner_key, -4.0, 4.0, (half_count, NOBS), jnp.float32)
    partner = -0.6 * leading + 0.8 * partner_own
    values = jnp.concatenate([leading, partner], axis=0)
    return values.astype(jnp.bfloat16)


def draw_valid_reading_numbers(key, part):
    values = jax.random.randint(key, (NOB,), 3 * OBW // 4, OBW + 1)
    return values.at[0].set(OBW).at[NOB - 1].set(1).astype(jnp.int32)


def draw_neighbour_lists(key, part):
    ncand = 3 * OB_DEV

    def one_block(block):
        subkey = jax.random.fold_in(key, block)
        ranked = jax.random.permutation(subkey, ncand).astype(jnp.int32)
        tile_no = block // CB_DEV
        candidates = (tile_no - 1) * OB_DEV + jnp.arange(ncand, dtype=jnp.int32)
        outside = ((candidates < 0) | (candidates >= NOB)).astype(jnp.int32)
        ordering = outside * (4 * ncand) + ranked
        ordering = jnp.where((block == 0) & (candidates == 0), -1, ordering)
        ordering = jnp.where((block == NCB - 1) & (candidates == NOB - 1), -1, ordering)
        order_idx = jnp.argsort(ordering, stable=True)
        return candidates[order_idx[:NLOC]].astype(jnp.int32)
    return jax.vmap(one_block)(jnp.arange(NCB, dtype=jnp.int32))


def levels(rng, extent, shards, least, largest):
    level = 1.0
    for dim, shards_of in shards:
        heights = jax.random.uniform(jax.random.fold_in(jax.random.fold_in(rng, 6), dim), (shards_of,), jnp.float32, least / len(shards), largest / len(shards))
        level = level * jnp.repeat(jnp.exp(heights), extent[dim] // shards_of).reshape((-1,) + (1,) * (len(extent) - 1 - dim))
    return level


def centred(rng, shape, deviation, bound, shards=(), kind=jnp.bfloat16):
    entries = jax.random.normal(rng, shape, jnp.float32) * deviation
    if len(shards) > 0:
        entries = levels(rng, shape, shards, -0.22, 0.18) * entries
    return jnp.clip(entries, min=-bound, max=bound).astype(kind)


def setup_inputs(seed: int = 0) -> dict:
    keys = jax.random.split(jax.random.key(seed), 7)
    return {
        "prior_members": draw_prior_members(jax.random.fold_in(keys[6], 71), 0),
        "members_in_reading_space": draw_members_in_reading_space(jax.random.fold_in(keys[6], 71), 0),
        "measured_values": centred(keys[2], (NOBS,), 1.0, 6.0, ((0, 16),), jnp.float32),
        "obs_precision_weights": jnp.clip(jnp.exp(math.log(4.0) - 2.0794415 * jax.random.uniform(keys[3], (NOBS,), jnp.float32) ** levels(keys[3], (NOBS,), ((0, 16),), -0.2, 0.2)), 0.5, 4.0),
        "valid_reading_numbers": draw_valid_reading_numbers(jax.random.fold_in(keys[6], 71), 0),
        "neighbour_lists": draw_neighbour_lists(jax.random.fold_in(keys[6], 71), 0),
    }


def newton_block(matrix):
    order = matrix.shape[0]
    eye = jnp.eye(order, dtype=jnp.float32)
    scale = jnp.trace(matrix) / order
    iterate = matrix / scale
    inverse_root = eye
    for step in range(NSTEPS):
        factor = 1.5 * eye - 0.5 * jnp.dot(inverse_root, iterate, precision=lax.Precision.HIGHEST)
        iterate = jnp.dot(iterate, factor, precision=lax.Precision.HIGHEST)
        inverse_root = jnp.dot(factor, inverse_root, precision=lax.Precision.HIGHEST)
    return (inverse_root, scale)

def transform(ylocal, wlocal, dlocal):
    order = ylocal.shape[0]
    scaled = (ylocal.astype(jnp.float32) * wlocal).astype(jnp.bfloat16)
    matrix = (order - 1.0) * jnp.eye(order, dtype=jnp.float32) + jnp.dot(scaled, ylocal.T, preferred_element_type=jnp.float32)
    rhs = jnp.dot(scaled.astype(jnp.float32), dlocal, precision=lax.Precision.HIGHEST)
    inverse_root, scale = newton_block(matrix)
    covar = jnp.dot(inverse_root, inverse_root, precision=lax.Precision.HIGHEST) / scale
    mean_shift = jnp.dot(covar, rhs, precision=lax.Precision.HIGHEST)
    return (jnp.sqrt((order - 1.0) / scale) * inverse_root + mean_shift[:, None]).astype(jnp.bfloat16)

def reference(prior_members, members_in_reading_space, measured_values, obs_precision_weights, valid_reading_numbers, neighbour_lists):
    prior_average = lax.optimization_barrier(jnp.mean(prior_members.astype(jnp.float32), axis=0))
    prior_deviation = (prior_members.astype(jnp.float32) - prior_average).astype(jnp.bfloat16)
    ymean = lax.optimization_barrier(jnp.mean(members_in_reading_space.astype(jnp.float32), axis=0))
    ypert = (members_in_reading_space.astype(jnp.float32) - ymean).astype(jnp.bfloat16)
    innov = measured_values - ymean
    slots = jnp.arange(OBW, dtype=jnp.int32)
    valid = slots[None, :] < valid_reading_numbers[:, None]
    weight = jnp.where(valid, obs_precision_weights.reshape(NOB, OBW), 0.0)
    yblocks = ypert.reshape(MEMBER_NUMBER, NOB, OBW)
    iblocks = innov.reshape(NOB, OBW)

    def per_block(ids):
        ylocal = yblocks[:, ids].reshape(MEMBER_NUMBER, NLOC * OBW)
        return transform(ylocal, weight[ids].reshape(NLOC * OBW), iblocks[ids].reshape(NLOC * OBW))
    weights = lax.map(per_block, neighbour_lists)
    pieces = prior_deviation.reshape(MEMBER_NUMBER, HEIGHT_LAYERS, NCB, CBW).astype(jnp.float32)
    mixed = jnp.einsum('ilbc,bij->jlbc', pieces, weights.astype(jnp.float32))
    return (prior_average + mixed.reshape(MEMBER_NUMBER, HEIGHT_LAYERS, GRID_POINTS)).astype(jnp.bfloat16)
```

```python
import functools

import jax
import jax.numpy as jnp
from jax import lax
from jax.experimental import pallas as pl
from jax.experimental.pallas import tpu as pltpu
from jax.sharding import PartitionSpec as P

NSTEPS = 3
CHUNKS = 4
VMEM_BYTES = 40 * 2**20
ANY = pl.BlockSpec(memory_space=pl.ANY)


def params(**kw):
    return pltpu.CompilerParams(vmem_limit_bytes=VMEM_BYTES, **kw)


def gather_kernel(nloc, ids_ref, low_ref, own_ref, high_ref, *rest):
    *outs, sems = rest
    width = outs[0].shape[2] // nloc
    blocks = own_ref.shape[1] // width
    base = 0
    for i, dst in enumerate(outs):

        def start(k, carry, dst=dst, i=i, base=base):
            b = k // nloc
            n = k - b * nloc
            g = ids_ref[base * nloc + k]
            t = g // blocks
            o = pl.multiple_of((g - t * blocks) * width, width)
            to = dst.at[b, :, pl.ds(pl.multiple_of(n * width, width), width)]
            for s, src in enumerate((low_ref, own_ref, high_ref)):

                @pl.when(t == s)
                def _():
                    pltpu.make_async_copy(src.at[:, pl.ds(o, width)], to, sems.at[i]).start()

            return carry

        lax.fori_loop(0, dst.shape[0] * nloc, start, 0)
        base += dst.shape[0]
    for i, dst in enumerate(outs):
        pltpu.make_async_copy(dst, dst, sems.at[i]).wait()


def gather(ids, low, own, high, counts, nloc, width):
    rows = own.shape[0]
    return pl.pallas_call(
        functools.partial(gather_kernel, nloc),
        out_shape=[jax.ShapeDtypeStruct((c, rows, nloc * width), own.dtype) for c in counts],
        grid_spec=pltpu.PrefetchScalarGridSpec(
            num_scalar_prefetch=1,
            grid=(1,),
            in_specs=[ANY] * 3,
            out_specs=[ANY] * len(counts),
            scratch_shapes=[pltpu.SemaphoreType.DMA((len(counts),))],
        ),
        compiler_params=params(),
    )(ids, low, own, high)


def matrix_kernel(nloc, ids_ref, mine_ref, peer_ref, side_ref, a_ref, rhs_ref):
    i = pl.program_id(0)
    rows = side_ref.shape[0] // 2
    y1 = mine_ref[0].astype(jnp.float32)
    y2 = peer_ref[0].astype(jnp.float32)
    members = 2 * y1.shape[0]
    mean = (jnp.sum(y1, 0, keepdims=True) + jnp.sum(y2, 0, keepdims=True)) * (1.0 / members)
    yp = jnp.concatenate([y1 - mean, y2 - mean], 0).astype(jnp.bfloat16)
    ids = [ids_ref[i * nloc + n] for n in range(nloc)]
    w = jnp.concatenate([side_ref[pl.ds(g, 1), :] for g in ids], 1)
    d = jnp.concatenate([side_ref[pl.ds(g + rows, 1), :] for g in ids], 1) - mean
    scaled = (yp.astype(jnp.float32) * w).astype(jnp.bfloat16)
    a = lax.dot_general(scaled, yp, (((1,), (1,)), ((), ())), preferred_element_type=jnp.float32)
    r = lax.broadcasted_iota(jnp.int32, a.shape, 0)
    c = lax.broadcasted_iota(jnp.int32, a.shape, 1)
    a_ref[0] = a + jnp.where(r == c, members - 1.0, 0.0)
    rhs_ref[0] = jnp.sum(scaled.astype(jnp.float32) * d, 1, keepdims=True)


def matrices(ids, mine, peer, side, first, nloc):
    count, rows, wide = peer.shape
    members = 2 * rows
    return pl.pallas_call(
        functools.partial(matrix_kernel, nloc),
        out_shape=[
            jax.ShapeDtypeStruct((count, members, members), jnp.float32),
            jax.ShapeDtypeStruct((count, members, 1), jnp.float32),
        ],
        grid_spec=pltpu.PrefetchScalarGridSpec(
            num_scalar_prefetch=1,
            grid=(count,),
            in_specs=[
                pl.BlockSpec((1, rows, wide), lambda i, s: (first + i, 0, 0)),
                pl.BlockSpec((1, rows, wide), lambda i, s: (i, 0, 0)),
                pl.BlockSpec(side.shape, lambda i, s: (0, 0)),
            ],
            out_specs=[
                pl.BlockSpec((1, members, members), lambda i, s: (i, 0, 0)),
                pl.BlockSpec((1, members, 1), lambda i, s: (i, 0, 0)),
            ],
        ),
        compiler_params=params(),
        cost_estimate=pl.CostEstimate(
            flops=2 * count * members * members * wide,
            bytes_accessed=count * members * wide * 4,
            transcendentals=0,
        ),
    )(ids, mine, peer, side)


def newton(matrix, rhs):
    members = matrix.shape[1]
    hi = lax.Precision.HIGHEST
    mm = functools.partial(jnp.einsum, "bij,bjk->bik", precision=hi)
    eye = jnp.eye(members, dtype=jnp.float32)
    scale = jnp.trace(matrix, axis1=1, axis2=2)[:, None, None] / members
    iterate = matrix / scale
    root = 1.5 * eye - 0.5 * iterate
    iterate = mm(iterate, root)
    for step in range(1, NSTEPS):
        factor = 1.5 * eye - 0.5 * mm(root, iterate)
        if step < NSTEPS - 1:
            iterate = mm(iterate, factor)
        root = mm(factor, root)
    half = jnp.sum(root * jnp.swapaxes(rhs, 1, 2), 2)
    shift = jnp.sum(root * half[:, None, :], 2) / scale[:, :, 0]
    turned = jnp.sqrt((members - 1.0) / scale) * jnp.swapaxes(root, 1, 2) + shift[:, None, :]
    return turned.astype(jnp.bfloat16)


def mix_kernel(where_ref, x1_ref, x2_ref, t_ref, *rest):
    res_ref, send_ref = rest[-2:]
    layers, rows, cols = x1_ref.shape
    means, devs = [], []
    for l in range(layers):
        a = x1_ref[l].astype(jnp.float32)
        b = x2_ref[l].astype(jnp.float32)
        m = (jnp.sum(a, 0, keepdims=True) + jnp.sum(b, 0, keepdims=True)) * (0.5 / rows)
        means.append(m)
        devs.append(jnp.concatenate([a - m, b - m], 0).astype(jnp.bfloat16))
    out = jnp.dot(t_ref[0], jnp.concatenate(devs, 1), preferred_element_type=jnp.float32)
    for l in range(layers):
        part = (out[:, l * cols:(l + 1) * cols] + means[l]).astype(res_ref.dtype)
        res_ref[l] = part[:rows]
        send_ref[l] = part[rows:]


def mix(where, prior, other, trans, res, first, cols):
    layers, rows, _ = prior.shape
    count = trans.shape[0]
    members = 2 * rows
    block = (layers, rows, cols)
    extra = [] if res is None else [res]
    here = lambda i, s: (0, 0, s[0] + first + i)
    return pl.pallas_call(
        mix_kernel,
        out_shape=[
            jax.ShapeDtypeStruct(prior.shape, prior.dtype),
            jax.ShapeDtypeStruct((layers, rows, count * cols), prior.dtype),
        ],
        grid_spec=pltpu.PrefetchScalarGridSpec(
            num_scalar_prefetch=1,
            grid=(count,),
            in_specs=[
                pl.BlockSpec(block, here),
                pl.BlockSpec(block, lambda i, s: (0, 0, first + i)),
                pl.BlockSpec((1, members, members), lambda i, s: (i, 0, 0)),
            ]
            + [ANY] * len(extra),
            out_specs=[pl.BlockSpec(block, here), pl.BlockSpec(block, lambda i, s: (0, 0, i))],
        ),
        input_output_aliases={4: 0} if extra else {},
        compiler_params=params(),
        cost_estimate=pl.CostEstimate(
            flops=2 * count * members * members * layers * cols,
            bytes_accessed=count * members * layers * cols * 4,
            transcendentals=0,
        ),
    )(where, prior, other, trans, *extra)


def place_kernel(first, cols, where_ref, got_ref, _, res_ref, sem):
    at = pl.multiple_of((where_ref[0] + first) * cols, cols)
    copy = pltpu.make_async_copy(got_ref, res_ref.at[:, :, pl.ds(at, got_ref.shape[2])], sem)
    copy.start()
    copy.wait()


def place(where, got, res, first, cols):
    return pl.pallas_call(
        functools.partial(place_kernel, first, cols),
        out_shape=jax.ShapeDtypeStruct(res.shape, res.dtype),
        grid_spec=pltpu.PrefetchScalarGridSpec(
            num_scalar_prefetch=1,
            grid=(1,),
            in_specs=[ANY, ANY],
            out_specs=ANY,
            scratch_shapes=[pltpu.SemaphoreType.DMA],
        ),
        input_output_aliases={2: 0},
        compiler_params=params(),
    )(where, got, res)


def per_device(prior, mapped, measured, precision, valid_numbers, lists):
    tile_no = lax.axis_index("tile")
    mem_no = lax.axis_index("mem")
    tiles = lax.axis_size("tile")
    forward = [(i, i + 1) for i in range(tiles - 1)]
    backward = [(b, a) for a, b in forward]
    swap = [(0, 1), (1, 0)]
    blocks = valid_numbers.shape[0]
    width = mapped.shape[1] // blocks
    col_blocks, nloc = lists.shape
    cols = prior.shape[2] // col_blocks
    half = col_blocks // 2
    per = half // CHUNKS

    slots = jnp.arange(width, dtype=jnp.int32)
    weight = jnp.where(
        slots[None, :] < valid_numbers[:, None], precision.reshape(blocks, width), 0.0
    )
    side = jnp.stack([weight, measured.reshape(blocks, width)])
    side_low = lax.ppermute(side, "tile", forward)
    side_high = lax.ppermute(side, "tile", backward)
    low = lax.ppermute(mapped, "tile", forward)
    high = lax.ppermute(mapped, "tile", backward)
    planes = jnp.transpose(prior, (1, 0, 2))
    other = lax.ppermute(
        lax.dynamic_slice_in_dim(planes, (1 - mem_no) * half * cols, half * cols, 2), "mem", swap
    )
    side = jnp.concatenate([side_low, side, side_high], 1).reshape(-1, width)

    ids = lists - (tile_no - 1) * blocks
    own_ids = lax.dynamic_slice_in_dim(ids, mem_no * half, half, 0).reshape(-1)
    peer_ids = lax.dynamic_slice_in_dim(ids, (1 - mem_no) * half, half, 0).reshape(-1)
    *out_y, mine = gather(
        jnp.concatenate([peer_ids, own_ids]), low, mapped, high, [per] * CHUNKS + [half], nloc, width
    )
    here = (mem_no * half).astype(jnp.int32).reshape(1)
    there = ((1 - mem_no) * half).astype(jnp.int32).reshape(1)
    in_y = [lax.ppermute(y, "mem", swap) for y in out_y]
    res, got = None, []
    for c in range(CHUNKS):
        first = c * per
        a, rhs = matrices(own_ids[first * nloc:(first + per) * nloc], mine, in_y[c], side, first, nloc)
        trans = newton(a, rhs)
        res, send = mix(here, planes, other, trans, res, first, cols)
        got.append(lax.ppermute(send, "mem", swap))
    for c in range(CHUNKS):
        res = place(there, got[c], res, c * per, cols)
    return jnp.transpose(res, (1, 0, 2))


def solution(mesh):
    in_specs = (
        P("mem", None, "tile"),
        P("mem", "tile"),
        P("tile"),
        P("tile"),
        P("tile"),
        P("tile", None),
    )
    return jax.shard_map(
        per_device, mesh=mesh, in_specs=in_specs, out_specs=P("mem", None, "tile"), check_vma=False
    )
```

```python
import functools

import jax
import jax.numpy as jnp
from jax import lax
from jax.experimental import pallas as pl
from jax.experimental.pallas import tpu as pltpu
from jax.sharding import PartitionSpec as P

NSTEPS = 3
CHUNKS = 4
VMEM_BYTES = 40 * 2**20
ANY = pl.BlockSpec(memory_space=pl.ANY)


def params(**kw):
    return pltpu.CompilerParams(vmem_limit_bytes=VMEM_BYTES, **kw)


def gather_kernel(nloc, ids_ref, low_ref, own_ref, high_ref, *rest):
    *outs, sems = rest
    width = outs[0].shape[2] // nloc
    blocks = own_ref.shape[1] // width
    base = 0
    for i, dst in enumerate(outs):

        def start(k, carry, dst=dst, i=i, base=base):
            b = k // nloc
            n = k - b * nloc
            g = ids_ref[base * nloc + k]
            t = g // blocks
            o = pl.multiple_of((g - t * blocks) * width, width)
            to = dst.at[b, :, pl.ds(pl.multiple_of(n * width, width), width)]
            for s, src in enumerate((low_ref, own_ref, high_ref)):

                @pl.when(t == s)
                def _():
                    pltpu.make_async_copy(src.at[:, pl.ds(o, width)], to, sems.at[i]).start()

            return carry

        lax.fori_loop(0, dst.shape[0] * nloc, start, 0)
        base += dst.shape[0]
    for i, dst in enumerate(outs):
        pltpu.make_async_copy(dst, dst, sems.at[i]).wait()


def gather(ids, low, own, high, counts, nloc, width):
    rows = own.shape[0]
    return pl.pallas_call(
        functools.partial(gather_kernel, nloc),
        out_shape=[jax.ShapeDtypeStruct((c, rows, nloc * width), own.dtype) for c in counts],
        grid_spec=pltpu.PrefetchScalarGridSpec(
            num_scalar_prefetch=1,
            grid=(1,),
            in_specs=[ANY] * 3,
            out_specs=[ANY] * len(counts),
            scratch_shapes=[pltpu.SemaphoreType.DMA((len(counts),))],
        ),
        compiler_params=params(),
    )(ids, low, own, high)


def matrix_kernel(nloc, ids_ref, mine_ref, peer_ref, side_ref, a_ref, rhs_ref):
    i = pl.program_id(0)
    rows = side_ref.shape[0] // 2
    y1 = mine_ref[0].astype(jnp.float32)
    y2 = peer_ref[0].astype(jnp.float32)
    members = 2 * y1.shape[0]
    mean = (jnp.sum(y1, 0, keepdims=True) + jnp.sum(y2, 0, keepdims=True)) * (1.0 / members)
    yp = jnp.concatenate([y1 - mean, y2 - mean], 0).astype(jnp.bfloat16)
    ids = [ids_ref[i * nloc + n] for n in range(nloc)]
    w = jnp.concatenate([side_ref[pl.ds(g, 1), :] for g in ids], 1)
    d = jnp.concatenate([side_ref[pl.ds(g + rows, 1), :] for g in ids], 1) - mean
    scaled = (yp.astype(jnp.float32) * w).astype(jnp.bfloat16)
    a = lax.dot_general(scaled, yp, (((1,), (1,)), ((), ())), preferred_element_type=jnp.float32)
    r = lax.broadcasted_iota(jnp.int32, a.shape, 0)
    c = lax.broadcasted_iota(jnp.int32, a.shape, 1)
    a_ref[0] = a + jnp.where(r == c, members - 1.0, 0.0)
    rhs_ref[0] = jnp.sum(scaled.astype(jnp.float32) * d, 1, keepdims=True)


def matrices(ids, mine, peer, side, first, nloc):
    count, rows, wide = peer.shape
    members = 2 * rows
    return pl.pallas_call(
        functools.partial(matrix_kernel, nloc),
        out_shape=[
            jax.ShapeDtypeStruct((count, members, members), jnp.float32),
            jax.ShapeDtypeStruct((count, members, 1), jnp.float32),
        ],
        grid_spec=pltpu.PrefetchScalarGridSpec(
            num_scalar_prefetch=1,
            grid=(count,),
            in_specs=[
                pl.BlockSpec((1, rows, wide), lambda i, s: (first + i, 0, 0)),
                pl.BlockSpec((1, rows, wide), lambda i, s: (i, 0, 0)),
                pl.BlockSpec(side.shape, lambda i, s: (0, 0)),
            ],
            out_specs=[
                pl.BlockSpec((1, members, members), lambda i, s: (i, 0, 0)),
                pl.BlockSpec((1, members, 1), lambda i, s: (i, 0, 0)),
            ],
        ),
        compiler_params=params(),
        cost_estimate=pl.CostEstimate(
            flops=2 * count * members * members * wide,
            bytes_accessed=count * members * wide * 4,
            transcendentals=0,
        ),
    )(ids, mine, peer, side)


def newton(matrix, rhs):
    members = matrix.shape[1]
    hi = lax.Precision.HIGHEST
    mm = functools.partial(jnp.einsum, "bij,bjk->bik", precision=hi)
    eye = jnp.eye(members, dtype=jnp.float32)
    scale = jnp.trace(matrix, axis1=1, axis2=2)[:, None, None] / members
    iterate = matrix / scale
    root = 1.5 * eye - 0.5 * iterate
    iterate = mm(iterate, root)
    for step in range(1, NSTEPS):
        factor = 1.5 * eye - 0.5 * mm(root, iterate)
        if step < NSTEPS - 1:
            iterate = mm(iterate, factor)
        root = mm(factor, root)
    half = jnp.sum(root * jnp.swapaxes(rhs, 1, 2), 2)
    shift = jnp.sum(root * half[:, None, :], 2) / scale[:, :, 0]
    turned = jnp.sqrt((members - 1.0) / scale) * jnp.swapaxes(root, 1, 2) + shift[:, None, :]
    return turned.astype(jnp.bfloat16)


def mix_kernel(where_ref, x1_ref, x2a_ref, x2b_ref, t_ref, *rest):
    res_ref, send_ref = rest[-2:]
    layers, rows, cols = x1_ref.shape
    means, devs = [], []
    for l in range(layers):
        a = x1_ref[l].astype(jnp.float32)
        split = x2a_ref.shape[0]
        b = (x2a_ref[l] if l < split else x2b_ref[l - split]).astype(jnp.float32)
        m = (jnp.sum(a, 0, keepdims=True) + jnp.sum(b, 0, keepdims=True)) * (0.5 / rows)
        means.append(m)
        devs.append(jnp.concatenate([a - m, b - m], 0).astype(jnp.bfloat16))
    out = jnp.dot(t_ref[0], jnp.concatenate(devs, 1), preferred_element_type=jnp.float32)
    for l in range(layers):
        part = (out[:, l * cols:(l + 1) * cols] + means[l]).astype(res_ref.dtype)
        res_ref[l] = part[:rows]
        send_ref[l] = part[rows:]


def mix(where, prior, others, trans, res, first, cols):
    layers, rows, _ = prior.shape
    count = trans.shape[0]
    members = 2 * rows
    block = (layers, rows, cols)
    extra = [] if res is None else [res]
    here = lambda i, s: (0, 0, s[0] + first + i)
    return pl.pallas_call(
        mix_kernel,
        out_shape=[
            jax.ShapeDtypeStruct(prior.shape, prior.dtype),
            jax.ShapeDtypeStruct((layers, rows, count * cols), prior.dtype),
        ],
        grid_spec=pltpu.PrefetchScalarGridSpec(
            num_scalar_prefetch=1,
            grid=(count,),
            in_specs=[
                pl.BlockSpec(block, here),
                *[
                    pl.BlockSpec((o.shape[0], rows, cols), lambda i, s: (0, 0, first + i))
                    for o in others
                ],
                pl.BlockSpec((1, members, members), lambda i, s: (i, 0, 0)),
            ]
            + [ANY] * len(extra),
            out_specs=[pl.BlockSpec(block, here), pl.BlockSpec(block, lambda i, s: (0, 0, i))],
        ),
        input_output_aliases={5: 0} if extra else {},
        compiler_params=params(),
        cost_estimate=pl.CostEstimate(
            flops=2 * count * members * members * layers * cols,
            bytes_accessed=count * members * layers * cols * 4,
            transcendentals=0,
        ),
    )(where, prior, *others, trans, *extra)


def place_kernel(first, cols, where_ref, got_ref, _, res_ref, sem):
    at = pl.multiple_of((where_ref[0] + first) * cols, cols)
    copy = pltpu.make_async_copy(got_ref, res_ref.at[:, :, pl.ds(at, got_ref.shape[2])], sem)
    copy.start()
    copy.wait()


def place(where, got, res, first, cols):
    return pl.pallas_call(
        functools.partial(place_kernel, first, cols),
        out_shape=jax.ShapeDtypeStruct(res.shape, res.dtype),
        grid_spec=pltpu.PrefetchScalarGridSpec(
            num_scalar_prefetch=1,
            grid=(1,),
            in_specs=[ANY, ANY],
            out_specs=ANY,
            scratch_shapes=[pltpu.SemaphoreType.DMA],
        ),
        input_output_aliases={2: 0},
        compiler_params=params(),
    )(where, got, res)


def per_device(prior, mapped, measured, precision, valid_numbers, lists):
    tile_no = lax.axis_index("tile")
    mem_no = lax.axis_index("mem")
    tiles = lax.axis_size("tile")
    forward = [(i, i + 1) for i in range(tiles - 1)]
    backward = [(b, a) for a, b in forward]
    swap = [(0, 1), (1, 0)]
    blocks = valid_numbers.shape[0]
    width = mapped.shape[1] // blocks
    col_blocks, nloc = lists.shape
    cols = prior.shape[2] // col_blocks
    half = col_blocks // 2
    per = half // CHUNKS

    slots = jnp.arange(width, dtype=jnp.int32)
    weight = jnp.where(
        slots[None, :] < valid_numbers[:, None], precision.reshape(blocks, width), 0.0
    )
    side = jnp.stack([weight, measured.reshape(blocks, width)])
    side_low = lax.ppermute(side, "tile", forward)
    side_high = lax.ppermute(side, "tile", backward)
    low = lax.ppermute(mapped, "tile", forward)
    high = lax.ppermute(mapped, "tile", backward)
    planes = jnp.transpose(prior, (1, 0, 2))
    layers, rows, _ = planes.shape
    split = layers * 4 // 5
    at = (1 - mem_no) * half * cols
    first_send = lax.dynamic_slice(planes, (0, 0, at), (split, rows, half * cols))
    last_send = lax.dynamic_slice(planes, (split, 0, at), (layers - split, rows, half * cols))
    others = [lax.ppermute(first_send, "mem", swap), lax.ppermute(last_send, "mem", swap)]
    low, high, side_low, side_high, others[0] = lax.optimization_barrier(
        (low, high, side_low, side_high, others[0])
    )
    side = jnp.concatenate([side_low, side, side_high], 1).reshape(-1, width)

    ids = lists - (tile_no - 1) * blocks
    own_ids = lax.dynamic_slice_in_dim(ids, mem_no * half, half, 0).reshape(-1)
    peer_ids = lax.dynamic_slice_in_dim(ids, (1 - mem_no) * half, half, 0).reshape(-1)
    *out_y, mine = gather(
        jnp.concatenate([peer_ids, own_ids]), low, mapped, high, [per] * CHUNKS + [half], nloc, width
    )
    here = (mem_no * half).astype(jnp.int32).reshape(1)
    there = ((1 - mem_no) * half).astype(jnp.int32).reshape(1)
    in_y = []
    for c, y in enumerate(out_y):
        if c > 1:
            y, in_y[c - 2] = lax.optimization_barrier((y, in_y[c - 2]))
        in_y.append(lax.ppermute(y, "mem", swap))
    res, got, send = None, [], None
    for c in range(CHUNKS):
        first = c * per
        y = in_y[c]
        if c > 0:
            y, _ = lax.optimization_barrier((y, send))
        a, rhs = matrices(own_ids[first * nloc:(first + per) * nloc], mine, y, side, first, nloc)
        trans = newton(a, rhs)
        if c > 1:
            res = place(there, got[c - 2], res, (c - 2) * per, cols)
        res, send = mix(here, planes, others, trans, res, first, cols)
        got.append(lax.ppermute(send, "mem", swap))
    for c in range(max(CHUNKS - 2, 0), CHUNKS):
        res = place(there, got[c], res, c * per, cols)
    return jnp.transpose(res, (1, 0, 2))


def solution(mesh):
    in_specs = (
        P("mem", None, "tile"),
        P("mem", "tile"),
        P("tile"),
        P("tile"),
        P("tile"),
        P("tile", None),
    )
    return jax.shard_map(
        per_device, mesh=mesh, in_specs=in_specs, out_specs=P("mem", None, "tile"), check_vma=False
    )
```
